32 devices in a mesh: groups: 2 (over y), rows: 4 (over z), sub: 4 (over x, core).
Axes of the slice: x: 2, y: 2, z: 4, core: 2. Of those that a mesh axis runs over, the one named last changes fastest.
Arguments:
- embeds: bfloat16 [32768, 256], P(('groups', 'rows')), parts along dimension 0, may hold values from -6 to 6
- start: float32 [64, 32768], P(None, ('groups', 'rows', 'sub')), parts along dimension 1, may hold values from -6 to 6
- pair_blocks: int32 [8, 4, 4, 2], P(('groups', 'rows'), 'sub'), parts along dimension 0, may hold values from 0 to 7, as said below
- pair_live: int32 [8, 4, 4], P(('groups', 'rows'), 'sub'), parts along dimension 0, may hold values from 0 to 1
Outputs:
- eigen_block: float32 [64, 32768], P(None, ('groups', 'rows', 'sub')), parts along dimension 1
The draws below stay inside these ranges and needn't reach their ends.
There are 2 independent parts, one for each index of `groups`. The reference program is written for one: setup_inputs(seed, part) draws one part's arguments, and reference() takes and returns one part's arrays. A program takes and returns all parts, laid end to end along the dimension named above; each array names one. Nothing has to cross between parts.
Inputs may be any that keep to these rules, and one draw needn't show every extreme that they name: `pair_blocks`: every entry is a local block index. Where the destination t equals the rows index r, the partner block differs from the owner block. Every block of every rows index is the owner block of some slot with pair_live 1.
All inputs are finite; a program needn't handle non-finite values.
Results may differ from the reference program's by a relative error of at most 0.014.
The reference program's roundings to bfloat16 on the way count: a program that leaves them out, or rounds other values in their place, can miss the bound.
Values may be sent and summed in bfloat16 or wider, within the bound.
A program may use at most 128 MiB of HBM per device.

```python
import math
import jax
import jax.numpy as jnp
from jax import lax

FEAT = 256
K = 64
BLOCK = 512
BLK_DEV = 8
ITERS = 1
ROWS_ALL = 16384
N_ROWS = 4
N_SUB = 4


def slot_numbers():
    sub_ids = jnp.arange(N_SUB, dtype=jnp.int32)[None, :, None]
    dest_ids = jnp.arange(N_ROWS, dtype=jnp.int32)[None, None, :]
    return sub_ids * N_ROWS + dest_ids


def draw_pair_blocks(key, part):
    first, second, third = jax.random.split(jax.random.fold_in(key, 11), 3)
    shape = (N_ROWS, N_SUB, N_ROWS)
    owners = jax.random.randint(first, shape, 0, BLK_DEV, dtype=jnp.int32)
    numbers = slot_numbers()
    owners = jnp.where(numbers < BLK_DEV, numbers, owners)
    partners = jax.random.randint(second, shape, 0, BLK_DEV, dtype=jnp.int32)
    same = jnp.arange(N_ROWS, dtype=jnp.int32)[:, None, None] == jnp.arange(N_ROWS, dtype=jnp.int32)[None, None, :]
    moved = (owners + 1 + jax.random.randint(third, shape, 0, BLK_DEV - 1, dtype=jnp.int32)) % BLK_DEV
    partners = jnp.where(same, moved, partners)
    return jnp.stack([owners, partners], axis=-1).astype(jnp.int32)


def draw_pair_live(key, part):
    first, second = jax.random.split(jax.random.fold_in(key, 23), 2)
    level = jax.random.randint(first, (N_ROWS, N_SUB, 1), 2, 9, dtype=jnp.int32)
    roll = jax.random.randint(second, (N_ROWS, N_SUB, N_ROWS), 0, 8, dtype=jnp.int32)
    live = (roll < level).astype(jnp.int32)
    return jnp.where(slot_numbers() < BLK_DEV, 1, live).astype(jnp.int32)


def shard_levels(own_key, shape, cuts, least, largest):
    level = 1.0
    for axis_at, shards_of in cuts:
        draws = jax.random.uniform(jax.random.fold_in(jax.random.fold_in(own_key, 6), axis_at), (shards_of,), jnp.float32, least / len(cuts), largest / len(cuts))
        level = level * jnp.repeat(jnp.exp(draws), shape[axis_at] // shards_of).reshape((-1,) + (1,) * (len(shape) - 1 - axis_at))
    return level


def normal_values(stream_key, extent, width, most, shards=(), kind=jnp.bfloat16):
    array = jax.random.normal(stream_key, extent, jnp.float32) * width
    if len(shards) > 0:
        array = shard_levels(stream_key, extent, shards, -0.22, 0.18) * array
    return jnp.clip(array, min=-most, max=most).astype(kind)


def setup_inputs(seed: int = 0, part: int = 0) -> dict:
    key_list = jax.random.split(jax.random.key(seed), 5)
    part_keys = jax.random.split(jax.random.fold_in(key_list[4], part), 5)
    embeds = normal_values(part_keys[0], (ROWS_ALL, FEAT), 1.0, 6.0, ((0, 4),))
    start = normal_values(part_keys[1], (K, ROWS_ALL), 1.0, 6.0, ((1, 16),), jnp.float32)
    pair_blocks = draw_pair_blocks(jax.random.fold_in(jax.random.fold_in(key_list[4], part), 71), part)
    pair_live = draw_pair_live(jax.random.fold_in(jax.random.fold_in(key_list[4], part), 71), part)
    return {"embeds": embeds, "start": start, "pair_blocks": pair_blocks, "pair_live": pair_live}


def unit_rows(embeds):
    values = embeds.astype(jnp.float32)
    scale = lax.rsqrt(lax.optimization_barrier(jnp.mean(values * values, axis=1, keepdims=True)) + 1e-05)
    return (values * scale * values.shape[1] ** (-0.5)).astype(jnp.bfloat16)

def add_range(total, begin, values):
    axis = total.ndim - 1
    current = lax.dynamic_slice_in_dim(total, begin, BLOCK, axis)
    return lax.dynamic_update_slice_in_dim(total, current + values, begin, axis)

def reference(embeds, start, pair_blocks, pair_live):
    units = unit_rows(embeds)
    sharpness = 2.0 * math.sqrt(FEAT)
    device_ids = jnp.arange(N_ROWS, dtype=jnp.int32)
    owner_rows = ((device_ids[:, None, None] * BLK_DEV + pair_blocks[..., 0]) * BLOCK).reshape(-1).astype(jnp.int32)
    partner_rows = ((device_ids[None, None, :] * BLK_DEV + pair_blocks[..., 1]) * BLOCK).reshape(-1).astype(jnp.int32)
    live_flags = pair_live.reshape(-1).astype(jnp.float32)

    def tile_at(owner, partner, flag):
        left = lax.dynamic_slice_in_dim(units, owner, BLOCK, 0)
        right = lax.dynamic_slice_in_dim(units, partner, BLOCK, 0)
        scores = jnp.dot(left.astype(jnp.float32), right.T.astype(jnp.float32), preferred_element_type=jnp.float32)
        return (jnp.exp(sharpness * scores) * flag).astype(jnp.bfloat16)

    def degree_step(degree, slot):
        owner, partner, flag = slot
        tile = tile_at(owner, partner, flag)
        degree = add_range(degree, owner, lax.optimization_barrier(jnp.sum(tile, axis=1, dtype=jnp.float32)))
        degree = add_range(degree, partner, lax.optimization_barrier(jnp.sum(tile, axis=0, dtype=jnp.float32)))
        return (degree, None)
    slots = (owner_rows, partner_rows, live_flags)
    degree, _ = lax.scan(degree_step, jnp.zeros((ROWS_ALL,), jnp.float32), slots)
    scaling = lax.rsqrt(degree)
    basis = start
    for step in range(ITERS):
        scaled = (basis * scaling[None, :]).astype(jnp.bfloat16)

        def apply_step(products, slot):
            owner, partner, flag = slot
            tile = tile_at(owner, partner, flag)
            partner_z = lax.dynamic_slice_in_dim(scaled, partner, BLOCK, 1)
            owner_z = lax.dynamic_slice_in_dim(scaled, owner, BLOCK, 1)
            products = add_range(products, owner, jnp.dot(partner_z.astype(jnp.float32), tile.T.astype(jnp.float32), preferred_element_type=jnp.float32))
            products = add_range(products, partner, jnp.dot(owner_z.astype(jnp.float32), tile.astype(jnp.float32), preferred_element_type=jnp.float32))
            return (products, None)
        products, _ = lax.scan(apply_step, jnp.zeros((K, ROWS_ALL), jnp.float32), slots)
        image = products * scaling[None, :]
        gram = jnp.dot(image.astype(jnp.float32), image.T.astype(jnp.float32), precision=lax.Precision.HIGHEST, preferred_element_type=jnp.float32)
        lower = jnp.linalg.cholesky(gram)
        basis = lax.linalg.triangular_solve(lower, image, left_side=True, lower=True)
    return basis * math.sqrt(ROWS_ALL)
```

```python
import functools
import math

import jax
import jax.numpy as jnp
from jax import lax
from jax.experimental import pallas as pl
from jax.experimental.pallas import tpu as pltpu
from jax.sharding import PartitionSpec as P

BLOCK = 512
MESH = pl.DeviceIdType.MESH
HIGH = lax.Precision.HIGHEST
F32 = jnp.float32
BF16 = jnp.bfloat16
IDS, UNITS, SUMS, SCALED, GUEST, GRAM_ROWS = range(6)
START, DEGREE, PRODUCTS, GRAM_SUB = range(4)


def each(count, body, first=0):
    if count <= 4:
        for i in range(first, count):
            body(i)
    else:

        def step(i, carry):
            body(i)
            return carry

        lax.fori_loop(first, count, step, 0)


def dot_t(left, right, **kw):
    return lax.dot_general(
        left, right, (((1,), (1,)), ((), ())), preferred_element_type=F32, **kw
    )


def subspace_kernel(
    slots, shares, own_ref, live_ref, ids_ref, embeds_ref, start_ref, image_ref, gram_ref,
    got_ids, served, units, sent_units, partner_units, tiles, col_sums, own_sums, got_sums,
    got_degree, degree_out, got_start, scaled, sent_scaled, partner_scaled, sent_guest, got_guest,
    owner_part, sent_products, got_products, gram_out, got_gram_sub, gram_part, got_gram_rows,
    row_send, row_recv, sub_send, sub_recv, local_sem,
):
    me_row = lax.axis_index("rows")
    me_sub = lax.axis_index("sub")
    blocks = units.shape[0]
    feat = units.shape[2]
    per_sub = blocks // shares
    other_row = lambda d: lax.rem(me_row + d, slots)
    other_sub = lambda d: lax.rem(me_sub + d, shares)

    def row_copy(kind, src, dst, at, arrives):
        return pltpu.make_async_remote_copy(
            src_ref=src, dst_ref=dst, send_sem=row_send.at[kind, at], recv_sem=row_recv.at[kind, arrives],
            device_id={"rows": at}, device_id_type=MESH,
        )

    def sub_copy(kind, src, dst, at, arrives):
        return pltpu.make_async_remote_copy(
            src_ref=src, dst_ref=dst, send_sem=sub_send.at[kind, at], recv_sem=sub_recv.at[kind, arrives],
            device_id={"sub": at}, device_id_type=MESH,
        )

    barrier = pltpu.get_barrier_semaphore()

    def greet_row(d):
        pl.semaphore_signal(barrier, inc=1, device_id={"rows": other_row(d)}, device_id_type=MESH)

    def greet_sub(d):
        pl.semaphore_signal(barrier, inc=1, device_id={"sub": other_sub(d)}, device_id_type=MESH)

    each(slots, greet_row, 1)
    each(shares, greet_sub, 1)
    pl.semaphore_wait(barrier, slots + shares - 2)

    each(slots, lambda d: row_copy(IDS, ids_ref.at[other_row(d)], got_ids.at[me_row], other_row(d), me_row).start(), 1)
    each(shares, lambda d: sub_copy(START, start_ref, got_start.at[me_sub], other_sub(d), me_sub).start(), 1)
    got_ids[me_row] = ids_ref[me_row]

    def normalise(j, carry):
        values = embeds_ref[pl.ds(pl.multiple_of(j * BLOCK, BLOCK), BLOCK), :].astype(F32)
        scale = lax.rsqrt(jnp.mean(values * values, axis=1, keepdims=True) + 1e-05)
        units[j] = (values * scale * feat ** (-0.5)).astype(BF16)
        return carry

    lax.fori_loop(0, blocks, normalise, 0)
    got_start[me_sub] = start_ref[...]

    each(slots, lambda d: row_copy(IDS, ids_ref.at[me_row], got_ids.at[other_row(d)], other_row(d), other_row(d)).wait_recv(), 1)
    to_scalar = pltpu.make_async_copy(got_ids, served, local_sem)
    to_scalar.start()
    to_scalar.wait()

    def serve_units(d):
        t = other_row(d)
        sent_units[t] = units[served[t, 0, 0]]
        row_copy(UNITS, sent_units.at[t], partner_units.at[me_row], t, me_row).start()

    each(slots, serve_units, 1)
    partner_units[me_row] = units[served[me_row, 0, 0]]

    sharpness = 2.0 * math.sqrt(feat)
    ones = jnp.ones((16, BLOCK), BF16)

    def build(d):
        t = other_row(d)
        if not (isinstance(d, int) and d == 0):
            row_copy(UNITS, sent_units.at[t], partner_units.at[t], t, t).wait_recv()
        live = live_ref[t].astype(F32)
        rows = 128

        def part(i, carry):
            at = pl.ds(pl.multiple_of(i * rows, rows), rows)
            scores = dot_t(units[own_ref[t], at, :], partner_units[t])
            tiles[t, at, :] = (jnp.exp(sharpness * scores) * live).astype(BF16)
            return carry

        lax.fori_loop(0, BLOCK // rows, part, 0)
        tile = tiles[t]
        col_sums[t] = jnp.dot(ones, tile, preferred_element_type=F32)[0:1]
        own_sums[t] = dot_t(ones, tile)[0:1]

    def build_and_send(d):
        t = other_row(d)
        build(d)
        row_copy(SUMS, col_sums.at[t], got_sums.at[me_row], t, me_row).start()

    build(0)
    got_sums[me_row] = col_sums[me_row]
    each(slots, build_and_send, 1)

    which = lax.broadcasted_iota(jnp.int32, (blocks, BLOCK), 0)
    degree_out[...] = jnp.zeros_like(degree_out)

    def fold_own(d):
        t = other_row(d)
        degree_out[...] += jnp.where(which == own_ref[t], own_sums[t], 0.0)

    def fold_served(d):
        t = other_row(d)
        if not (isinstance(d, int) and d == 0):
            row_copy(SUMS, col_sums.at[t], got_sums.at[t], t, t).wait_recv()
        degree_out[...] += jnp.where(which == served[t, 0, 0], got_sums[t], 0.0)

    fold_own(0)
    each(slots, fold_own, 1)
    fold_served(0)
    each(slots, fold_served, 1)
    each(shares, lambda d: sub_copy(DEGREE, degree_out, got_degree.at[me_sub], other_sub(d), me_sub).start(), 1)
    got_degree[me_sub] = degree_out[...]
    each(shares, lambda d: sub_copy(DEGREE, degree_out, got_degree.at[other_sub(d)], other_sub(d), other_sub(d)).wait_recv(), 1)
    inverse = lax.rsqrt(jnp.sum(got_degree[...], axis=0))

    each(shares, lambda d: sub_copy(START, start_ref, got_start.at[other_sub(d)], other_sub(d), other_sub(d)).wait_recv(), 1)
    for j in range(blocks):
        at = (j % per_sub) * BLOCK
        scaled[j] = (got_start[j // per_sub, :, at : at + BLOCK] * inverse[j : j + 1]).astype(BF16)

    def serve_scaled(d):
        t = other_row(d)
        sent_scaled[t] = scaled[served[t, 0, 0]]
        row_copy(SCALED, sent_scaled.at[t], partner_scaled.at[me_row], t, me_row).start()

    each(slots, serve_scaled, 1)
    partner_scaled[me_row] = scaled[served[me_row, 0, 0]]

    def outward(d):
        t = other_row(d)
        sent_guest[t] = jnp.dot(scaled[own_ref[t]], tiles[t], preferred_element_type=F32).astype(BF16)
        row_copy(GUEST, sent_guest.at[t], got_guest.at[me_row], t, me_row).start()

    each(slots, outward, 1)
    got_guest[me_row] = jnp.dot(scaled[own_ref[me_row]], tiles[me_row], preferred_element_type=F32).astype(BF16)
    owner_part[me_row] = dot_t(partner_scaled[me_row], tiles[me_row])

    def inward(d):
        t = other_row(d)
        row_copy(SCALED, sent_scaled.at[t], partner_scaled.at[t], t, t).wait_recv()
        owner_part[t] = dot_t(partner_scaled[t], tiles[t])

    each(slots, inward, 1)
    each(slots, lambda d: row_copy(GUEST, sent_guest.at[other_row(d)], got_guest.at[other_row(d)], other_row(d), other_row(d)).wait_recv(), 1)

    def total_of(j):
        total = jnp.zeros(owner_part.shape[1:], F32)

        def add(t, total):
            mine = jnp.where(own_ref[t] == j, 1.0, 0.0)
            guest = jnp.where(served[t, 0, 0] == j, 1.0, 0.0)
            return total + mine * owner_part[t] + guest * got_guest[t].astype(F32)

        if slots <= 4:
            for t in range(slots):
                total = add(t, total)
            return total
        return lax.fori_loop(0, slots, add, total)

    def share(d):
        to = other_sub(d)
        for b in range(per_sub):
            sent_products[to, :, b * BLOCK : (b + 1) * BLOCK] = total_of(to * per_sub + b).astype(BF16)
        sub_copy(PRODUCTS, sent_products.at[to], got_products.at[me_sub], to, me_sub).start()

    each(shares, share, 1)
    for b in range(per_sub):
        got_products[me_sub, :, b * BLOCK : (b + 1) * BLOCK] = total_of(me_sub * per_sub + b).astype(BF16)
    each(shares, lambda d: sub_copy(PRODUCTS, sent_products.at[me_sub], got_products.at[other_sub(d)], other_sub(d), other_sub(d)).wait_recv(), 1)

    for b in range(per_sub):
        cols = slice(b * BLOCK, (b + 1) * BLOCK)
        products = jnp.sum(got_products[:, :, cols].astype(F32), axis=0)
        mine = jnp.sum(jnp.where(which == me_sub * per_sub + b, inverse, 0.0), axis=0, keepdims=True)
        image_ref[:, cols] = products * mine
    image = image_ref[...]
    local = dot_t(image, image, precision=HIGH)
    gram_out[...] = local
    each(shares, lambda d: sub_copy(GRAM_SUB, gram_out, got_gram_sub.at[me_sub], other_sub(d), me_sub).start(), 1)
    got_gram_sub[me_sub] = local
    each(shares, lambda d: sub_copy(GRAM_SUB, gram_out, got_gram_sub.at[other_sub(d)], other_sub(d), other_sub(d)).wait_recv(), 1)
    part_sum = jnp.sum(got_gram_sub[...], axis=0)
    gram_part[...] = part_sum
    each(slots, lambda d: row_copy(GRAM_ROWS, gram_part, got_gram_rows.at[me_row], other_row(d), me_row).start(), 1)
    got_gram_rows[me_row] = part_sum
    each(slots, lambda d: row_copy(GRAM_ROWS, gram_part, got_gram_rows.at[other_row(d)], other_row(d), other_row(d)).wait_recv(), 1)
    gram_ref[...] = jnp.sum(got_gram_rows[...], axis=0)

    def sent_along_rows(d):
        t = other_row(d)
        row_copy(IDS, ids_ref.at[t], got_ids.at[me_row], t, me_row).wait_send()
        row_copy(UNITS, sent_units.at[t], partner_units.at[me_row], t, me_row).wait_send()
        row_copy(SUMS, col_sums.at[t], got_sums.at[me_row], t, me_row).wait_send()
        row_copy(SCALED, sent_scaled.at[t], partner_scaled.at[me_row], t, me_row).wait_send()
        row_copy(GUEST, sent_guest.at[t], got_guest.at[me_row], t, me_row).wait_send()
        row_copy(GRAM_ROWS, gram_part, got_gram_rows.at[me_row], t, me_row).wait_send()

    def sent_along_sub(d):
        to = other_sub(d)
        sub_copy(START, start_ref, got_start.at[me_sub], to, me_sub).wait_send()
        sub_copy(DEGREE, degree_out, got_degree.at[me_sub], to, me_sub).wait_send()
        sub_copy(PRODUCTS, sent_products.at[to], got_products.at[me_sub], to, me_sub).wait_send()
        sub_copy(GRAM_SUB, gram_out, got_gram_sub.at[me_sub], to, me_sub).wait_send()

    each(slots, sent_along_rows, 1)
    each(shares, sent_along_sub, 1)


def basis_kernel(size, gram_ref, image_ref, out_ref):
    width = gram_ref.shape[0]
    row = lax.broadcasted_iota(jnp.int32, (width, width), 0)
    col = lax.broadcasted_iota(jnp.int32, (width, width), 1)
    work = jnp.concatenate([gram_ref[...], jnp.where(row == col, 1.0, 0.0)], axis=1)
    below = lax.broadcasted_iota(jnp.int32, (width, 1), 0)
    for j in range(width):
        factor = jnp.where(below > j, work[:, j : j + 1] / work[j : j + 1, j : j + 1], 0.0)
        work = work - factor * work[j : j + 1, :]
    pivots = jnp.sum(jnp.where(row == col, work[:, :width], 0.0), axis=1, keepdims=True)
    lower_inverse = work[:, width:] * (lax.rsqrt(pivots) * size)
    out_ref[...] = jnp.dot(lower_inverse, image_ref[...], precision=HIGH, preferred_element_type=F32)


def per_device(embeds, start, pair_blocks, pair_live):
    slots = lax.axis_size("rows")
    shares = lax.axis_size("sub")
    width, cols = start.shape
    rows_dev, feat = embeds.shape
    blocks = rows_dev // BLOCK
    own_ids = pair_blocks[0, 0, :, 0]
    partner_ids = jnp.broadcast_to(pair_blocks[0, 0, :, 1][:, None, None], (slots, 1, 128))
    vmem = pl.BlockSpec(memory_space=pltpu.VMEM)
    smem = pl.BlockSpec(memory_space=pltpu.SMEM)
    dma = pltpu.SemaphoreType.DMA
    image, gram = pl.pallas_call(
        functools.partial(subspace_kernel, slots, shares),
        out_shape=[
            jax.ShapeDtypeStruct((width, cols), F32),
            jax.ShapeDtypeStruct((width, width), F32),
        ],
        in_specs=[smem, smem, vmem, vmem, vmem],
        out_specs=[vmem, vmem],
        scratch_shapes=[
            pltpu.VMEM((slots, 1, 128), jnp.int32),
            pltpu.SMEM((slots, 1, 128), jnp.int32),
            pltpu.VMEM((blocks, BLOCK, feat), BF16),
            pltpu.VMEM((slots, BLOCK, feat), BF16),
            pltpu.VMEM((slots, BLOCK, feat), BF16),
            pltpu.VMEM((slots, BLOCK, BLOCK), BF16),
            pltpu.VMEM((slots, 1, BLOCK), F32),
            pltpu.VMEM((slots, 1, BLOCK), F32),
            pltpu.VMEM((slots, 1, BLOCK), F32),
            pltpu.VMEM((shares, blocks, BLOCK), F32),
            pltpu.VMEM((blocks, BLOCK), F32),
            pltpu.VMEM((shares, width, cols), F32),
            pltpu.VMEM((blocks, width, BLOCK), BF16),
            pltpu.VMEM((slots, width, BLOCK), BF16),
            pltpu.VMEM((slots, width, BLOCK), BF16),
            pltpu.VMEM((slots, width, BLOCK), BF16),
            pltpu.VMEM((slots, width, BLOCK), BF16),
            pltpu.VMEM((slots, width, BLOCK), F32),
            pltpu.VMEM((shares, width, cols), BF16),
            pltpu.VMEM((shares, width, cols), BF16),
            pltpu.VMEM((width, width), F32),
            pltpu.VMEM((shares, width, width), F32),
            pltpu.VMEM((width, width), F32),
            pltpu.VMEM((slots, width, width), F32),
            dma((6, slots)),
            dma((6, slots)),
            dma((4, shares)),
            dma((4, shares)),
            dma(()),
        ],
        compiler_params=pltpu.CompilerParams(
            collective_id=0, has_side_effects=True, vmem_limit_bytes=60 * 2**20
        ),
        name="subspace",
    )(own_ids, pair_live[0, 0], partner_ids, embeds, start)
    return pl.pallas_call(
        functools.partial(basis_kernel, math.sqrt(rows_dev * slots)),
        out_shape=jax.ShapeDtypeStruct((width, cols), F32),
        in_specs=[vmem, vmem],
        out_specs=vmem,
        compiler_params=pltpu.CompilerParams(vmem_limit_bytes=32 * 2**20),
        name="basis",
    )(gram, image)


def solution(mesh):
    placed = (
        P(("groups", "rows"), None),
        P(None, ("groups", "rows", "sub")),
        P(("groups", "rows"), "sub", None, None),
        P(("groups", "rows"), "sub", None),
    )
    return jax.shard_map(
        per_device,
        mesh=mesh,
        in_specs=placed,
        out_specs=P(None, ("groups", "rows", "sub")),
        check_vma=False,
    )
```

```python
import functools
import math

import jax
import jax.numpy as jnp
from jax import lax
from jax.experimental import pallas as pl
from jax.experimental.pallas import tpu as pltpu
from jax.sharding import PartitionSpec as P

BLOCK = 512
HALVES = 2
MESH = pl.DeviceIdType.MESH
HIGH = lax.Precision.HIGHEST
F32 = jnp.float32
BF16 = jnp.bfloat16
META, SUMS, SCALED, PRODUCT, GRAM_ROWS = range(5)
START, DEGREE, PRODUCTS, GRAM_SUB = range(4)


def each(count, body, first=0):
    if count <= 4:
        for i in range(first, count):
            body(i)
    else:

        def step(i, carry):
            body(i)
            return carry

        lax.fori_loop(first, count, step, 0)


def dot_t(left, right, **kw):
    return lax.dot_general(
        left, right, (((1,), (1,)), ((), ())), preferred_element_type=F32, **kw
    )


def subspace_kernel(
    slots, shares, pairs_ref, live_ref, embeds_hbm, start_hbm, image_ref, gram_ref,
    embeds, sent_meta, got_meta, served, units, sent_units, got_units, tiles, col_sums, own_sums, got_sums,
    got_degree, degree_out, got_start, scaled, sent_scaled, got_scaled, sent_product, got_product,
    local_part, sent_products, got_products, gram_out, got_gram_sub, gram_part, got_gram_rows,
    row_send, row_recv, unit_send, unit_recv, sub_send, sub_recv, local_sem,
):
    me_row = lax.axis_index("rows")
    me_sub = lax.axis_index("sub")
    blocks, _, feat = units.shape
    width = scaled.shape[1]
    per_sub = blocks // shares
    half = BLOCK // HALVES
    other_row = lambda d: lax.rem(me_row + d, slots)
    other_sub = lambda d: lax.rem(me_sub + d, shares)
    own = lambda t: pairs_ref[0, 0, t, 0]
    partner = lambda r: served[r, 0, 0]

    load_embeds = pltpu.make_async_copy(embeds_hbm, embeds, local_sem.at[0])
    load_embeds.start()
    load_start = pltpu.make_async_copy(start_hbm, got_start.at[me_sub], local_sem.at[1])
    load_start.start()

    def row_copy(kind, src, dst, at, arrives):
        return pltpu.make_async_remote_copy(
            src_ref=src, dst_ref=dst, send_sem=row_send.at[kind, at], recv_sem=row_recv.at[kind, arrives],
            device_id={"rows": at}, device_id_type=MESH,
        )

    def unit_copy(h, at, arrives):
        part = pl.ds(h * half, half)
        return pltpu.make_async_remote_copy(
            src_ref=sent_units.at[at, part], dst_ref=got_units.at[arrives, part],
            send_sem=unit_send.at[h, at], recv_sem=unit_recv.at[h, arrives],
            device_id={"rows": at}, device_id_type=MESH,
        )

    def sub_copy(kind, src, dst, at, arrives):
        return pltpu.make_async_remote_copy(
            src_ref=src, dst_ref=dst, send_sem=sub_send.at[kind, at], recv_sem=sub_recv.at[kind, arrives],
            device_id={"sub": at}, device_id_type=MESH,
        )

    barrier = pltpu.get_barrier_semaphore()

    def greet_row(d):
        pl.semaphore_signal(barrier, inc=1, device_id={"rows": other_row(d)}, device_id_type=MESH)

    def greet_sub(d):
        pl.semaphore_signal(barrier, inc=1, device_id={"sub": other_sub(d)}, device_id_type=MESH)

    each(slots, greet_row, 1)
    each(shares, greet_sub, 1)

    lane = lax.broadcasted_iota(jnp.int32, (1, 128), 1)

    def put_meta(d):
        t = other_row(d)
        sent_meta[t] = jnp.where(lane == 0, pairs_ref[0, 0, t, 1], live_ref[0, 0, t])

    each(slots, put_meta)

    def unit_rows(values):
        values = values.astype(F32)
        scale = lax.rsqrt(jnp.mean(values * values, axis=1, keepdims=True) + 1e-05)
        return (values * scale * feat ** (-0.5)).astype(BF16)

    load_embeds.wait()

    def fill(h, d):
        t = other_row(d)
        part = pl.ds(h * half, half)
        sent_units[t, part, :] = unit_rows(embeds[own(t), part, :])

    each(slots, lambda d: fill(0, d), 1)
    pl.semaphore_wait(barrier, slots + shares - 2)
    for h in range(HALVES):
        if h:
            each(slots, lambda d: fill(h, d), 1)
        each(slots, lambda d: unit_copy(h, other_row(d), me_row).start(), 1)
        if h == 0:
            each(slots, lambda d: row_copy(META, sent_meta.at[other_row(d)], got_meta.at[me_row], other_row(d), me_row).start(), 1)
    load_start.wait()
    each(shares, lambda d: sub_copy(START, got_start.at[me_sub], got_start.at[me_sub], other_sub(d), me_sub).start(), 1)
    got_meta[me_row] = sent_meta[me_row]

    def normalise(j, carry):
        units[j] = unit_rows(embeds[j])
        return carry

    lax.fori_loop(0, blocks, normalise, 0)
    got_units[me_row] = units[own(me_row)]

    each(slots, lambda d: row_copy(META, sent_meta.at[me_row], got_meta.at[other_row(d)], other_row(d), other_row(d)).wait_recv(), 1)
    to_scalar = pltpu.make_async_copy(got_meta, served, local_sem.at[2])
    to_scalar.start()
    to_scalar.wait()

    sharpness = 2.0 * math.sqrt(feat)
    ones = jnp.ones((16, BLOCK), BF16)
    rows = 128

    def build(h, d):
        r = other_row(d)
        remote = not (isinstance(d, int) and d == 0)
        if remote:
            unit_copy(h, me_row, r).wait_recv()
        live = served[r, 0, 1].astype(F32)

        def part(i, sums):
            at = pl.ds(pl.multiple_of(h * half + i * rows, rows), rows)
            scores = dot_t(got_units[r, at, :], units[partner(r)])
            tile = (jnp.exp(sharpness * scores) * live).astype(BF16)
            tiles[r, at, :] = tile
            return sums + jnp.sum(tile.astype(F32).reshape(rows // 8, 8, BLOCK), axis=0)

        sums = lax.fori_loop(0, half // rows, part, jnp.zeros((8, BLOCK), F32))
        sums = jnp.sum(sums, axis=0, keepdims=True)
        col_sums[r] = sums if h == 0 else col_sums[r] + sums
        if h == HALVES - 1:
            own_sums[r] = dot_t(ones, tiles[r])[0:1]
            if remote:
                row_copy(SUMS, own_sums.at[r], got_sums.at[me_row], r, me_row).start()

    for h in range(HALVES):
        build(h, 0)
    got_sums[me_row] = own_sums[me_row]
    for h in range(HALVES):
        each(slots, lambda d: build(h, d), 1)

    which = lax.broadcasted_iota(jnp.int32, (blocks, BLOCK), 0)
    degree_out[...] = jnp.zeros_like(degree_out)

    def fold_partner(d):
        r = other_row(d)
        degree_out[...] += jnp.where(which == partner(r), col_sums[r], 0.0)

    def fold_own(d):
        t = other_row(d)
        if not (isinstance(d, int) and d == 0):
            row_copy(SUMS, own_sums.at[t], got_sums.at[t], t, t).wait_recv()
        degree_out[...] += jnp.where(which == own(t), got_sums[t], 0.0)

    each(slots, fold_partner)
    fold_own(0)
    each(slots, fold_own, 1)
    each(shares, lambda d: sub_copy(DEGREE, degree_out, got_degree.at[me_sub], other_sub(d), me_sub).start(), 1)
    got_degree[me_sub] = degree_out[...]
    each(shares, lambda d: sub_copy(START, got_start.at[me_sub], got_start.at[other_sub(d)], other_sub(d), other_sub(d)).wait_recv(), 1)
    each(shares, lambda d: sub_copy(DEGREE, degree_out, got_degree.at[other_sub(d)], other_sub(d), other_sub(d)).wait_recv(), 1)
    inverse = lax.rsqrt(jnp.sum(got_degree[...], axis=0))

    for j in range(blocks):
        at = (j % per_sub) * BLOCK
        scaled[j] = (got_start[j // per_sub, :, at : at + BLOCK] * inverse[j : j + 1]).astype(BF16)

    def serve_scaled(d):
        t = other_row(d)
        sent_scaled[t] = scaled[own(t)]
        row_copy(SCALED, sent_scaled.at[t], got_scaled.at[me_row], t, me_row).start()

    each(slots, serve_scaled, 1)
    got_scaled[me_row] = scaled[own(me_row)]

    def back(d):
        r = other_row(d)
        sent_product[r] = dot_t(scaled[partner(r)], tiles[r]).astype(BF16)
        row_copy(PRODUCT, sent_product.at[r], got_product.at[me_row], r, me_row).start()

    each(slots, back, 1)
    got_product[me_row] = dot_t(scaled[partner(me_row)], tiles[me_row]).astype(BF16)

    def stay(d):
        r = other_row(d)
        if not (isinstance(d, int) and d == 0):
            row_copy(SCALED, sent_scaled.at[r], got_scaled.at[r], r, r).wait_recv()
        local_part[r] = jnp.dot(got_scaled[r], tiles[r], preferred_element_type=F32)

    stay(0)
    each(slots, stay, 1)
    each(slots, lambda d: row_copy(PRODUCT, sent_product.at[other_row(d)], got_product.at[other_row(d)], other_row(d), other_row(d)).wait_recv(), 1)

    def total_of(j):
        total = jnp.zeros(local_part.shape[1:], F32)

        def add(t, total):
            there = jnp.where(own(t) == j, 1.0, 0.0)
            here = jnp.where(partner(t) == j, 1.0, 0.0)
            return total + here * local_part[t] + there * got_product[t].astype(F32)

        if slots <= 4:
            for t in range(slots):
                total = add(t, total)
            return total
        return lax.fori_loop(0, slots, add, total)

    def share(d):
        to = other_sub(d)
        for b in range(per_sub):
            sent_products[to, :, b * BLOCK : (b + 1) * BLOCK] = total_of(to * per_sub + b).astype(BF16)
        sub_copy(PRODUCTS, sent_products.at[to], got_products.at[me_sub], to, me_sub).start()

    each(shares, share, 1)
    for b in range(per_sub):
        got_products[me_sub, :, b * BLOCK : (b + 1) * BLOCK] = total_of(me_sub * per_sub + b).astype(BF16)
    each(shares, lambda d: sub_copy(PRODUCTS, sent_products.at[me_sub], got_products.at[other_sub(d)], other_sub(d), other_sub(d)).wait_recv(), 1)

    for b in range(per_sub):
        cols = slice(b * BLOCK, (b + 1) * BLOCK)
        products = jnp.sum(got_products[:, :, cols].astype(F32), axis=0)
        mine = jnp.sum(jnp.where(which == me_sub * per_sub + b, inverse, 0.0), axis=0, keepdims=True)
        image_ref[:, cols] = products * mine
    image = image_ref[...]
    local = dot_t(image, image, precision=HIGH)
    local = jnp.concatenate([local[: width // 2], local[width // 2 :]], axis=1)
    gram_out[...] = local
    each(shares, lambda d: sub_copy(GRAM_SUB, gram_out, got_gram_sub.at[me_sub], other_sub(d), me_sub).start(), 1)
    got_gram_sub[me_sub] = local
    each(shares, lambda d: sub_copy(GRAM_SUB, gram_out, got_gram_sub.at[other_sub(d)], other_sub(d), other_sub(d)).wait_recv(), 1)
    part_sum = jnp.sum(got_gram_sub[...], axis=0)
    gram_part[...] = part_sum
    each(slots, lambda d: row_copy(GRAM_ROWS, gram_part, got_gram_rows.at[me_row], other_row(d), me_row).start(), 1)
    got_gram_rows[me_row] = part_sum
    each(slots, lambda d: row_copy(GRAM_ROWS, gram_part, got_gram_rows.at[other_row(d)], other_row(d), other_row(d)).wait_recv(), 1)
    gram_ref[...] = jnp.sum(got_gram_rows[...], axis=0)

    def sent_along_rows(d):
        t = other_row(d)
        row_copy(META, sent_meta.at[t], got_meta.at[me_row], t, me_row).wait_send()
        for h in range(HALVES):
            unit_copy(h, t, me_row).wait_send()
        row_copy(SUMS, own_sums.at[t], got_sums.at[me_row], t, me_row).wait_send()
        row_copy(SCALED, sent_scaled.at[t], got_scaled.at[me_row], t, me_row).wait_send()
        row_copy(PRODUCT, sent_product.at[t], got_product.at[me_row], t, me_row).wait_send()
        row_copy(GRAM_ROWS, gram_part, got_gram_rows.at[me_row], t, me_row).wait_send()

    def sent_along_sub(d):
        to = other_sub(d)
        sub_copy(START, got_start.at[me_sub], got_start.at[me_sub], to, me_sub).wait_send()
        sub_copy(DEGREE, degree_out, got_degree.at[me_sub], to, me_sub).wait_send()
        sub_copy(PRODUCTS, sent_products.at[to], got_products.at[me_sub], to, me_sub).wait_send()
        sub_copy(GRAM_SUB, gram_out, got_gram_sub.at[me_sub], to, me_sub).wait_send()

    each(slots, sent_along_rows, 1)
    each(shares, sent_along_sub, 1)


def basis_kernel(size, gram_ref, image_ref, out_ref):
    width = gram_ref.shape[0] * 2
    packed = gram_ref[...]
    gram = jnp.concatenate([packed[:, :width], packed[:, width:]], axis=0)
    row = lax.broadcasted_iota(jnp.int32, (width, width), 0)
    col = lax.broadcasted_iota(jnp.int32, (width, width), 1)
    work = jnp.concatenate([gram, jnp.where(row == col, 1.0, 0.0)], axis=1)
    below = lax.broadcasted_iota(jnp.int32, (width, 1), 0)
    for j in range(width):
        factor = jnp.where(below > j, work[:, j : j + 1] / work[j : j + 1, j : j + 1], 0.0)
        work = work - factor * work[j : j + 1, :]
    pivots = jnp.sum(jnp.where(row == col, work[:, :width], 0.0), axis=1, keepdims=True)
    lower_inverse = work[:, width:] * (lax.rsqrt(pivots) * size)
    out_ref[...] = jnp.dot(lower_inverse, image_ref[...], precision=HIGH, preferred_element_type=F32)


def per_device(embeds, start, pair_blocks, pair_live):
    slots = lax.axis_size("rows")
    shares = lax.axis_size("sub")
    width, cols = start.shape
    rows_dev, feat = embeds.shape
    blocks = rows_dev // BLOCK
    vmem = pl.BlockSpec(memory_space=pltpu.VMEM)
    smem = pl.BlockSpec(memory_space=pltpu.SMEM)
    dma = pltpu.SemaphoreType.DMA
    image, gram = pl.pallas_call(
        functools.partial(subspace_kernel, slots, shares),
        out_shape=[
            jax.ShapeDtypeStruct((width, cols), F32),
            jax.ShapeDtypeStruct((width // 2, 2 * width), F32),
        ],
        in_specs=[smem, smem, pl.BlockSpec(memory_space=pl.ANY), pl.BlockSpec(memory_space=pl.ANY)],
        out_specs=[vmem, vmem],
        scratch_shapes=[
            pltpu.VMEM((blocks, BLOCK, feat), BF16),
            pltpu.VMEM((slots, 1, 128), jnp.int32),
            pltpu.VMEM((slots, 1, 128), jnp.int32),
            pltpu.SMEM((slots, 1, 128), jnp.int32),
            pltpu.VMEM((blocks, BLOCK, feat), BF16),
            pltpu.VMEM((slots, BLOCK, feat), BF16),
            pltpu.VMEM((slots, BLOCK, feat), BF16),
            pltpu.VMEM((slots, BLOCK, BLOCK), BF16),
            pltpu.VMEM((slots, 1, BLOCK), F32),
            pltpu.VMEM((slots, 1, BLOCK), F32),
            pltpu.VMEM((slots, 1, BLOCK), F32),
            pltpu.VMEM((shares, blocks, BLOCK), F32),
            pltpu.VMEM((blocks, BLOCK), F32),
            pltpu.VMEM((shares, width, cols), F32),
            pltpu.VMEM((blocks, width, BLOCK), BF16),
            pltpu.VMEM((slots, width, BLOCK), BF16),
            pltpu.VMEM((slots, width, BLOCK), BF16),
            pltpu.VMEM((slots, width, BLOCK), BF16),
            pltpu.VMEM((slots, width, BLOCK), BF16),
            pltpu.VMEM((slots, width, BLOCK), F32),
            pltpu.VMEM((shares, width, cols), BF16),
            pltpu.VMEM((shares, width, cols), BF16),
            pltpu.VMEM((width // 2, 2 * width), F32),
            pltpu.VMEM((shares, width // 2, 2 * width), F32),
            pltpu.VMEM((width // 2, 2 * width), F32),
            pltpu.VMEM((slots, width // 2, 2 * width), F32),
            dma((5, slots)),
            dma((5, slots)),
            dma((HALVES, slots)),
            dma((HALVES, slots)),
            dma((4, shares)),
            dma((4, shares)),
            dma((3,)),
        ],
        compiler_params=pltpu.CompilerParams(
            collective_id=0, has_side_effects=True, vmem_limit_bytes=60 * 2**20
        ),
        name="subspace",
    )(pair_blocks, pair_live, embeds.reshape(blocks, BLOCK, feat), start)
    return pl.pallas_call(
        functools.partial(basis_kernel, math.sqrt(rows_dev * slots)),
        out_shape=jax.ShapeDtypeStruct((width, cols), F32),
        in_specs=[vmem, vmem],
        out_specs=vmem,
        compiler_params=pltpu.CompilerParams(vmem_limit_bytes=32 * 2**20),
        name="basis",
    )(gram, image)


def solution(mesh):
    placed = (
        P(("groups", "rows"), None),
        P(None, ("groups", "rows", "sub")),
        P(("groups", "rows"), "sub", None, None),
        P(("groups", "rows"), "sub", None),
    )
    return jax.shard_map(
        per_device,
        mesh=mesh,
        in_specs=placed,
        out_specs=P(None, ("groups", "rows", "sub")),
        check_vma=False,
    )
```

```python
import functools
import math

import jax
import jax.numpy as jnp
from jax import lax
from jax.experimental import pallas as pl
from jax.experimental.pallas import tpu as pltpu
from jax.sharding import PartitionSpec as P

BLOCK = 512
HALVES = 2
MESH = pl.DeviceIdType.MESH
HIGH = lax.Precision.HIGHEST
F32 = jnp.float32
BF16 = jnp.bfloat16
META, SUMS, SCALED, PRODUCT, GRAM_ROWS = range(5)
START, DEGREE, PRODUCTS, GRAM_SUB = range(4)


def each(count, body, first=0):
    if count <= 4:
        for i in range(first, count):
            body(i)
    else:

        def step(i, carry):
            body(i)
            return carry

        lax.fori_loop(first, count, step, 0)


def dot_t(left, right, **kw):
    return lax.dot_general(
        left, right, (((1,), (1,)), ((), ())), preferred_element_type=F32, **kw
    )


def subspace_kernel(
    slots, shares, pairs_ref, live_ref, embeds_hbm, start_hbm, image_ref, gram_ref,
    embeds, sent_meta, got_meta, served, units, sent_units, got_units, tiles, col_sums, own_sums, got_sums,
    got_degree, degree_out, got_start, scaled, sent_scaled, got_scaled, sent_product, got_product,
    local_part, local_total, sent_products, got_products, gram_out, got_gram_sub, gram_part, got_gram_rows,
    row_send, row_recv, unit_send, unit_recv, sub_send, sub_recv, local_sem,
):
    me_row = lax.axis_index("rows")
    me_sub = lax.axis_index("sub")
    blocks, _, feat = units.shape
    width = scaled.shape[1]
    per_sub = blocks // shares
    half = BLOCK // HALVES
    other_row = lambda d: lax.rem(me_row + d, slots)
    other_sub = lambda d: lax.rem(me_sub + d, shares)
    own = lambda t: pairs_ref[0, 0, t, 0]
    partner = lambda r: served[r, 0, 0]

    load_embeds = pltpu.make_async_copy(embeds_hbm, embeds, local_sem.at[0])
    load_embeds.start()
    load_start = pltpu.make_async_copy(start_hbm, got_start.at[me_sub], local_sem.at[1])
    load_start.start()

    def row_copy(kind, src, dst, at, arrives):
        return pltpu.make_async_remote_copy(
            src_ref=src, dst_ref=dst, send_sem=row_send.at[kind, at], recv_sem=row_recv.at[kind, arrives],
            device_id={"rows": at}, device_id_type=MESH,
        )

    def unit_copy(h, at, arrives):
        part = pl.ds(h * half, half)
        return pltpu.make_async_remote_copy(
            src_ref=sent_units.at[at, part], dst_ref=got_units.at[arrives, part],
            send_sem=unit_send.at[h, at], recv_sem=unit_recv.at[h, arrives],
            device_id={"rows": at}, device_id_type=MESH,
        )

    def sub_copy(kind, src, dst, at, arrives):
        return pltpu.make_async_remote_copy(
            src_ref=src, dst_ref=dst, send_sem=sub_send.at[kind, at], recv_sem=sub_recv.at[kind, arrives],
            device_id={"sub": at}, device_id_type=MESH,
        )

    barrier = pltpu.get_barrier_semaphore()

    def greet_row(d):
        pl.semaphore_signal(barrier, inc=1, device_id={"rows": other_row(d)}, device_id_type=MESH)

    def greet_sub(d):
        pl.semaphore_signal(barrier, inc=1, device_id={"sub": other_sub(d)}, device_id_type=MESH)

    each(slots, greet_row, 1)
    each(shares, greet_sub, 1)

    lane = lax.broadcasted_iota(jnp.int32, (1, 128), 1)

    def put_meta(d):
        t = other_row(d)
        sent_meta[t] = jnp.where(lane == 0, pairs_ref[0, 0, t, 1], live_ref[0, 0, t])

    each(slots, put_meta)

    def unit_rows(values):
        values = values.astype(F32)
        scale = lax.rsqrt(jnp.mean(values * values, axis=1, keepdims=True) + 1e-05)
        return (values * scale * feat ** (-0.5)).astype(BF16)

    load_embeds.wait()

    def fill(h, d):
        t = other_row(d)
        part = pl.ds(h * half, half)
        sent_units[t, part, :] = unit_rows(embeds[own(t), part, :])

    each(slots, lambda d: fill(0, d), 1)
    pl.semaphore_wait(barrier, slots + shares - 2)
    for h in range(HALVES):
        if h:
            each(slots, lambda d: fill(h, d), 1)
        each(slots, lambda d: unit_copy(h, other_row(d), me_row).start(), 1)
        if h == 0:
            each(slots, lambda d: row_copy(META, sent_meta.at[other_row(d)], got_meta.at[me_row], other_row(d), me_row).start(), 1)
    load_start.wait()
    each(shares, lambda d: sub_copy(START, got_start.at[me_sub], got_start.at[me_sub], other_sub(d), me_sub).start(), 1)
    got_meta[me_row] = sent_meta[me_row]

    def normalise(j, carry):
        units[j] = unit_rows(embeds[j])
        return carry

    lax.fori_loop(0, blocks, normalise, 0)
    got_units[me_row] = units[own(me_row)]

    each(slots, lambda d: row_copy(META, sent_meta.at[me_row], got_meta.at[other_row(d)], other_row(d), other_row(d)).wait_recv(), 1)
    to_scalar = pltpu.make_async_copy(got_meta, served, local_sem.at[2])
    to_scalar.start()
    to_scalar.wait()

    sharpness = 2.0 * math.sqrt(feat)
    ones = jnp.ones((16, BLOCK), BF16)
    rows = 128

    def build(h, d):
        r = other_row(d)
        remote = not (isinstance(d, int) and d == 0)
        if remote:
            unit_copy(h, me_row, r).wait_recv()
        live = served[r, 0, 1].astype(F32)

        def part(i, sums):
            at = pl.ds(pl.multiple_of(h * half + i * rows, rows), rows)
            scores = dot_t(got_units[r, at, :], units[partner(r)])
            tile = (jnp.exp(sharpness * scores) * live).astype(BF16)
            tiles[r, at, :] = tile
            return sums + jnp.sum(tile.astype(F32).reshape(rows // 8, 8, BLOCK), axis=0)

        sums = lax.fori_loop(0, half // rows, part, jnp.zeros((8, BLOCK), F32))
        sums = jnp.sum(sums, axis=0, keepdims=True)
        col_sums[r] = sums if h == 0 else col_sums[r] + sums
        if h == HALVES - 1:
            own_sums[r] = dot_t(ones, tiles[r])[0:1]
            if remote:
                row_copy(SUMS, own_sums.at[r], got_sums.at[me_row], r, me_row).start()

    for h in range(HALVES):
        build(h, 0)
    got_sums[me_row] = own_sums[me_row]
    for h in range(HALVES):
        each(slots, lambda d: build(h, d), 1)

    which = lax.broadcasted_iota(jnp.int32, (blocks, BLOCK), 0)
    degree_out[...] = jnp.zeros_like(degree_out)

    def fold_partner(d):
        r = other_row(d)
        degree_out[...] += jnp.where(which == partner(r), col_sums[r], 0.0)

    def fold_own(d):
        t = other_row(d)
        if not (isinstance(d, int) and d == 0):
            row_copy(SUMS, own_sums.at[t], got_sums.at[t], t, t).wait_recv()
        degree_out[...] += jnp.where(which == own(t), got_sums[t], 0.0)

    each(slots, fold_partner)
    fold_own(0)
    each(slots, fold_own, 1)
    each(shares, lambda d: sub_copy(DEGREE, degree_out, got_degree.at[me_sub], other_sub(d), me_sub).start(), 1)
    got_degree[me_sub] = degree_out[...]
    each(shares, lambda d: sub_copy(START, got_start.at[me_sub], got_start.at[other_sub(d)], other_sub(d), other_sub(d)).wait_recv(), 1)
    each(shares, lambda d: sub_copy(DEGREE, degree_out, got_degree.at[other_sub(d)], other_sub(d), other_sub(d)).wait_recv(), 1)
    inverse = lax.rsqrt(jnp.sum(got_degree[...], axis=0))

    for j in range(blocks):
        at = (j % per_sub) * BLOCK
        scaled[j] = (got_start[j // per_sub, :, at : at + BLOCK] * inverse[j : j + 1]).astype(BF16)

    def serve_scaled(d):
        t = other_row(d)
        sent_scaled[t] = scaled[own(t)]
        row_copy(SCALED, sent_scaled.at[t], got_scaled.at[me_row], t, me_row).start()

    each(slots, serve_scaled, 1)
    got_scaled[me_row] = scaled[own(me_row)]

    def back(d):
        r = other_row(d)
        sent_product[r] = dot_t(scaled[partner(r)], tiles[r]).astype(BF16)
        row_copy(PRODUCT, sent_product.at[r], got_product.at[me_row], r, me_row).start()

    each(slots, back, 1)
    got_product[me_row] = dot_t(scaled[partner(me_row)], tiles[me_row]).astype(BF16)

    def stay(d):
        r = other_row(d)
        if not (isinstance(d, int) and d == 0):
            row_copy(SCALED, sent_scaled.at[r], got_scaled.at[r], r, r).wait_recv()
        local_part[r] = jnp.dot(got_scaled[r], tiles[r], preferred_element_type=F32)

    stay(0)
    each(slots, stay, 1)

    def sum_slots(total, add):
        if slots <= 4:
            for t in range(slots):
                total = add(t, total)
            return total
        return lax.fori_loop(0, slots, add, total)

    def fold_local(j, carry):
        add = lambda t, total: total + jnp.where(partner(t) == j, 1.0, 0.0) * local_part[t]
        local_total[j] = sum_slots(jnp.zeros(local_part.shape[1:], F32), add)
        return carry

    lax.fori_loop(0, blocks, fold_local, 0)
    each(slots, lambda d: row_copy(PRODUCT, sent_product.at[other_row(d)], got_product.at[other_row(d)], other_row(d), other_row(d)).wait_recv(), 1)

    def total_of(j):
        add = lambda t, total: total + jnp.where(own(t) == j, 1.0, 0.0) * got_product[t].astype(F32)
        return sum_slots(local_total[j], add)

    def share(d):
        to = other_sub(d)
        for b in range(per_sub):
            sent_products[to, :, b * BLOCK : (b + 1) * BLOCK] = total_of(to * per_sub + b).astype(BF16)
        sub_copy(PRODUCTS, sent_products.at[to], got_products.at[me_sub], to, me_sub).start()

    each(shares, share, 1)
    for b in range(per_sub):
        got_products[me_sub, :, b * BLOCK : (b + 1) * BLOCK] = total_of(me_sub * per_sub + b).astype(BF16)
    each(shares, lambda d: sub_copy(PRODUCTS, sent_products.at[me_sub], got_products.at[other_sub(d)], other_sub(d), other_sub(d)).wait_recv(), 1)

    for b in range(per_sub):
        cols = slice(b * BLOCK, (b + 1) * BLOCK)
        products = jnp.sum(got_products[:, :, cols].astype(F32), axis=0)
        mine = jnp.sum(jnp.where(which == me_sub * per_sub + b, inverse, 0.0), axis=0, keepdims=True)
        image_ref[:, cols] = products * mine
    image = image_ref[...]
    local = dot_t(image, image, precision=HIGH)
    local = jnp.concatenate([local[: width // 2], local[width // 2 :]], axis=1)
    gram_out[...] = local
    each(shares, lambda d: sub_copy(GRAM_SUB, gram_out, got_gram_sub.at[me_sub], other_sub(d), me_sub).start(), 1)
    got_gram_sub[me_sub] = local
    each(shares, lambda d: sub_copy(GRAM_SUB, gram_out, got_gram_sub.at[other_sub(d)], other_sub(d), other_sub(d)).wait_recv(), 1)
    part_sum = jnp.sum(got_gram_sub[...], axis=0)
    gram_part[...] = part_sum
    each(slots, lambda d: row_copy(GRAM_ROWS, gram_part, got_gram_rows.at[me_row], other_row(d), me_row).start(), 1)
    got_gram_rows[me_row] = part_sum
    each(slots, lambda d: row_copy(GRAM_ROWS, gram_part, got_gram_rows.at[other_row(d)], other_row(d), other_row(d)).wait_recv(), 1)
    gram_ref[...] = jnp.sum(got_gram_rows[...], axis=0)

    def sent_along_rows(d):
        t = other_row(d)
        row_copy(META, sent_meta.at[t], got_meta.at[me_row], t, me_row).wait_send()
        for h in range(HALVES):
            unit_copy(h, t, me_row).wait_send()
        row_copy(SUMS, own_sums.at[t], got_sums.at[me_row], t, me_row).wait_send()
        row_copy(SCALED, sent_scaled.at[t], got_scaled.at[me_row], t, me_row).wait_send()
        row_copy(PRODUCT, sent_product.at[t], got_product.at[me_row], t, me_row).wait_send()
        row_copy(GRAM_ROWS, gram_part, got_gram_rows.at[me_row], t, me_row).wait_send()

    def sent_along_sub(d):
        to = other_sub(d)
        sub_copy(START, got_start.at[me_sub], got_start.at[me_sub], to, me_sub).wait_send()
        sub_copy(DEGREE, degree_out, got_degree.at[me_sub], to, me_sub).wait_send()
        sub_copy(PRODUCTS, sent_products.at[to], got_products.at[me_sub], to, me_sub).wait_send()
        sub_copy(GRAM_SUB, gram_out, got_gram_sub.at[me_sub], to, me_sub).wait_send()

    each(slots, sent_along_rows, 1)
    each(shares, sent_along_sub, 1)


def basis_kernel(size, gram_ref, image_ref, out_ref):
    width = gram_ref.shape[0] * 2
    packed = gram_ref[...]
    gram = jnp.concatenate([packed[:, :width], packed[:, width:]], axis=0)
    row = lax.broadcasted_iota(jnp.int32, (width, width), 0)
    col = lax.broadcasted_iota(jnp.int32, (width, width), 1)
    work = jnp.concatenate([gram, jnp.where(row == col, 1.0, 0.0)], axis=1)
    below = lax.broadcasted_iota(jnp.int32, (width, 1), 0)
    for j in range(width):
        factor = jnp.where(below > j, work[:, j : j + 1] / work[j : j + 1, j : j + 1], 0.0)
        work = work - factor * work[j : j + 1, :]
    pivots = jnp.sum(jnp.where(row == col, work[:, :width], 0.0), axis=1, keepdims=True)
    lower_inverse = work[:, width:] * (lax.rsqrt(pivots) * size)
    out_ref[...] = jnp.dot(lower_inverse, image_ref[...], precision=HIGH, preferred_element_type=F32)


def per_device(embeds, start, pair_blocks, pair_live):
    slots = lax.axis_size("rows")
    shares = lax.axis_size("sub")
    width, cols = start.shape
    rows_dev, feat = embeds.shape
    blocks = rows_dev // BLOCK
    vmem = pl.BlockSpec(memory_space=pltpu.VMEM)
    smem = pl.BlockSpec(memory_space=pltpu.SMEM)
    dma = pltpu.SemaphoreType.DMA
    image, gram = pl.pallas_call(
        functools.partial(subspace_kernel, slots, shares),
        out_shape=[
            jax.ShapeDtypeStruct((width, cols), F32),
            jax.ShapeDtypeStruct((width // 2, 2 * width), F32),
        ],
        in_specs=[smem, smem, pl.BlockSpec(memory_space=pl.ANY), pl.BlockSpec(memory_space=pl.ANY)],
        out_specs=[vmem, vmem],
        scratch_shapes=[
            pltpu.VMEM((blocks, BLOCK, feat), BF16),
            pltpu.VMEM((slots, 1, 128), jnp.int32),
            pltpu.VMEM((slots, 1, 128), jnp.int32),
            pltpu.SMEM((slots, 1, 128), jnp.int32),
            pltpu.VMEM((blocks, BLOCK, feat), BF16),
            pltpu.VMEM((slots, BLOCK, feat), BF16),
            pltpu.VMEM((slots, BLOCK, feat), BF16),
            pltpu.VMEM((slots, BLOCK, BLOCK), BF16),
            pltpu.VMEM((slots, 1, BLOCK), F32),
            pltpu.VMEM((slots, 1, BLOCK), F32),
            pltpu.VMEM((slots, 1, BLOCK), F32),
            pltpu.VMEM((shares, blocks, BLOCK), F32),
            pltpu.VMEM((blocks, BLOCK), F32),
            pltpu.VMEM((shares, width, cols), F32),
            pltpu.VMEM((blocks, width, BLOCK), BF16),
            pltpu.VMEM((slots, width, BLOCK), BF16),
            pltpu.VMEM((slots, width, BLOCK), BF16),
            pltpu.VMEM((slots, width, BLOCK), BF16),
            pltpu.VMEM((slots, width, BLOCK), BF16),
            pltpu.VMEM((slots, width, BLOCK), F32),
            pltpu.VMEM((blocks, width, BLOCK), F32),
            pltpu.VMEM((shares, width, cols), BF16),
            pltpu.VMEM((shares, width, cols), BF16),
            pltpu.VMEM((width // 2, 2 * width), F32),
            pltpu.VMEM((shares, width // 2, 2 * width), F32),
            pltpu.VMEM((width // 2, 2 * width), F32),
            pltpu.VMEM((slots, width // 2, 2 * width), F32),
            dma((5, slots)),
            dma((5, slots)),
            dma((HALVES, slots)),
            dma((HALVES, slots)),
            dma((4, shares)),
            dma((4, shares)),
            dma((3,)),
        ],
        compiler_params=pltpu.CompilerParams(
            collective_id=0, has_side_effects=True, vmem_limit_bytes=60 * 2**20
        ),
        name="subspace",
    )(pair_blocks, pair_live, embeds.reshape(blocks, BLOCK, feat), start)
    return pl.pallas_call(
        functools.partial(basis_kernel, math.sqrt(rows_dev * slots)),
        out_shape=jax.ShapeDtypeStruct((width, cols), F32),
        in_specs=[vmem, vmem],
        out_specs=vmem,
        compiler_params=pltpu.CompilerParams(vmem_limit_bytes=32 * 2**20),
        name="basis",
    )(gram, image)


def solution(mesh):
    placed = (
        P(("groups", "rows"), None),
        P(None, ("groups", "rows", "sub")),
        P(("groups", "rows"), "sub", None, None),
        P(("groups", "rows"), "sub", None),
    )
    return jax.shard_map(
        per_device,
        mesh=mesh,
        in_specs=placed,
        out_specs=P(None, ("groups", "rows", "sub")),
        check_vma=False,
    )
```
